32 devices in a mesh: seq: 8 (over z, y), tensor: 4 (over x, core).
Axes of the slice: x: 2, y: 2, z: 4, core: 2. Of those that a mesh axis runs over, the one named last changes fastest.
Arguments:
- state: bfloat16 [8192, 2048], P('seq', 'tensor'), may hold values from -20.5 to 20.5
- memory: bfloat16 [128, 2048], P('seq', 'tensor'), may hold values from -20.5 to 20.5
- w_query: bfloat16 [2048, 2048], P('seq', 'tensor'), may hold values from -0.1875 to 0.1875
- w_key: bfloat16 [2048, 2048], P('seq', 'tensor'), may hold values from -0.1875 to 0.1875
- w_value: bfloat16 [2048, 2048], P('seq', 'tensor'), may hold values from -0.125 to 0.125
- w_output: bfloat16 [2048, 2048], P('tensor', 'seq'), may hold values from -0.375 to 0.375
- norm_gain: float32 [2048], P('tensor'), may hold values from 0.1 to 1.9
- remaining: int32 [8192], P('seq'), may hold values from 0 to 3
- slot_home: int32 [128], replicated, may hold values from 0 to 7
Outputs:
- new_state: bfloat16 [8192, 2048], P('seq', 'tensor')
- new_memory: bfloat16 [128, 2048], P('seq', 'tensor')
The draws below stay inside these ranges and needn't reach their ends.
Inputs may be any that keep to these rules, and one draw needn't show every extreme that they name: `remaining`: 0 means the token has halted.
All inputs are finite; a program needn't handle non-finite values.
Results may differ from the reference program's by a relative error of at most 0.014.
The reference program's roundings to bfloat16 on the way count: a program that leaves them out, or rounds other values in their place, can miss the bound.
Values may be sent and summed in bfloat16 or wider, within the bound.
A program may use at most 128 MiB of HBM per device.

```python
import math
import jax
import jax.numpy as jnp
from jax import lax

D = 2048
H = 16
HD = 128
HALF = 256
TOK_DEV = 1024
QB = 512
SEQ = 8192
MEM = 128
N_SEQ = 8
N_TENSOR = 4


def draw_rows(key, count):
    base_key = jax.random.fold_in(key, 0)
    return jnp.clip(jax.random.normal(base_key, (count, D), jnp.float32), -5.0, 5.0)


def draw_state(key, part):
    return draw_rows(jax.random.fold_in(key, 3), SEQ).astype(jnp.bfloat16)


def draw_memory(key, part):
    return draw_rows(jax.random.fold_in(key, 7), MEM).astype(jnp.bfloat16)


def place_ends(entries, own_key, smallest, high):
    shape = entries.shape
    place = [jax.random.randint(jax.random.fold_in(own_key, axis), (), 0, shape[axis]) for axis in range(len(shape))]
    entries = entries.at[tuple(place)].set(smallest)
    longest = shape.index(max(shape))
    place[longest] = (place[longest] + 1) % shape[longest]
    return entries.at[tuple(place)].set(high)


def level_of(key, dims, cuts, smallest, largest):
    loudness = 1.0
    for axis_at, shards_of in cuts:
        steps = jax.random.uniform(jax.random.fold_in(jax.random.fold_in(key, 6), axis_at), (shards_of,), jnp.float32, smallest / len(cuts), largest / len(cuts))
        loudness = loudness * jnp.repeat(jnp.exp(steps), dims[axis_at] // shards_of).reshape((-1,) + (1,) * (len(dims) - 1 - axis_at))
    return loudness


def gaussian(own_key, dims, deviation, bound, cuts=(), kind=jnp.bfloat16):
    values = jax.random.normal(own_key, dims, jnp.float32) * deviation
    if len(cuts) > 0:
        values = level_of(own_key, dims, cuts, -0.22, 0.18) * values
    return jnp.clip(values, min=-bound, max=bound).astype(kind)


def setup_inputs(seed: int = 0) -> dict:
    key_of = jax.random.split(jax.random.key(seed), 10)
    return {
        "state": draw_state(jax.random.fold_in(key_of[9], 71), 0),
        "memory": draw_memory(jax.random.fold_in(key_of[9], 71), 0),
        "w_query": gaussian(key_of[2], (D, D), (D // 2) ** -0.5, 0.1875, ((0, 8), (1, 4))),
        "w_key": gaussian(key_of[3], (D, D), (D // 2) ** -0.5, 0.1875, ((0, 8), (1, 4))),
        "w_value": gaussian(key_of[4], (D, D), D ** -0.5, 0.125, ((0, 8), (1, 4))),
        "w_output": gaussian(key_of[5], (D, D), (D // 8) ** -0.5, 0.375, ((0, 4), (1, 8))),
        "norm_gain": jnp.clip(1.0 + 0.18 * jax.random.normal(key_of[6], (D,), jnp.float32), 0.1, 1.9),
        "remaining": place_ends(jax.random.randint(key_of[7], (SEQ,), 0, 4), jax.random.fold_in(key_of[7], 1), 0, 3).astype(jnp.int32),
        "slot_home": place_ends(jax.random.randint(key_of[8], (MEM,), 0, N_SEQ), jax.random.fold_in(key_of[8], 1), 0, N_SEQ - 1).astype(jnp.int32),
    }


EPS = 1e-05
MASKED = -1e+30

def reference(state, memory, w_query, w_key, w_value, w_output, norm_gain, remaining, slot_home):
    rows = jnp.concatenate([state, memory], axis=0)
    query = jnp.dot(rows, w_query, preferred_element_type=jnp.float32).astype(jnp.bfloat16)
    keys = jnp.dot(rows, w_key, preferred_element_type=jnp.float32).astype(jnp.bfloat16)
    values = jnp.dot(rows, w_value, preferred_element_type=jnp.float32).astype(jnp.bfloat16)
    score_scale = 1.0 / math.sqrt(HD)
    distance_slopes = 0.25 * 8.0 ** (jnp.arange(H, dtype=jnp.int32).astype(jnp.float32) / (H - 1))
    homes = slot_home.astype(jnp.float32)
    tok_query = query[:SEQ].reshape(SEQ, H, HD)
    token_key_rows = keys[:SEQ].reshape(SEQ, H, HD)
    token_value_rows = values[:SEQ].reshape(SEQ, H, HD)
    memory_slot_query = query[SEQ:].reshape(MEM, H, HD).astype(jnp.float32)
    memory_slot_keys = keys[SEQ:].reshape(MEM, H, HD).astype(jnp.float32)
    memory_slot_values = values[SEQ:].reshape(MEM, H, HD).astype(jnp.float32)
    pad_keys = jnp.pad(token_key_rows, ((HALF, HALF), (0, 0), (0, 0)))
    pad_values = jnp.pad(token_value_rows, ((HALF, HALF), (0, 0), (0, 0)))
    window_extent = QB + 2 * HALF

    def token_block(number):
        start = number * QB
        query_matrix = lax.dynamic_slice_in_dim(tok_query, start, QB, 0).astype(jnp.float32)
        near_keys = lax.dynamic_slice_in_dim(pad_keys, start, window_extent, 0).astype(jnp.float32)
        near_values = lax.dynamic_slice_in_dim(pad_values, start, window_extent, 0).astype(jnp.float32)
        near = jnp.einsum('qhd,khd->hqk', query_matrix, near_keys) * score_scale
        qpos = start + jnp.arange(QB, dtype=jnp.int32)
        kpos = start - HALF + jnp.arange(window_extent, dtype=jnp.int32)
        valid = (jnp.abs(qpos[:, None] - kpos[None, :]) <= HALF) & (kpos >= 0)[None, :] & (kpos < SEQ)[None, :]
        near = jnp.where(valid[None], near, MASKED)
        blocks = (qpos // TOK_DEV).astype(jnp.float32)
        position_distances = jnp.abs(homes[None, :] - blocks[:, None])
        distant_mask = jnp.einsum('taw,caw->atc', query_matrix, memory_slot_keys) * score_scale - distance_slopes[:, None, None] * position_distances[None]
        scores = jnp.concatenate([near, distant_mask], axis=2)
        top = lax.optimization_barrier(jnp.max(scores, axis=2, keepdims=True))
        exponent_terms = jnp.exp(scores - top)
        total = lax.optimization_barrier(jnp.sum(exponent_terms, axis=2))
        attention_probabilities = lax.optimization_barrier(exponent_terms.astype(jnp.bfloat16)).astype(jnp.float32)
        both_values = jnp.concatenate([near_values, memory_slot_values], axis=0)
        numer = jnp.einsum('hqk,khd->qhd', attention_probabilities, both_values)
        return (numer / jnp.transpose(total)[:, :, None]).astype(jnp.bfloat16).reshape(QB, D)
    token_mix = lax.map(token_block, jnp.arange(SEQ // QB, dtype=jnp.int32)).reshape(SEQ, D)

    def slot_block(carry, number):
        best, den, num = carry
        start = number * TOK_DEV
        window_block_keys = lax.dynamic_slice_in_dim(token_key_rows, start, TOK_DEV, 0).astype(jnp.float32)
        window_block_values = lax.dynamic_slice_in_dim(token_value_rows, start, TOK_DEV, 0).astype(jnp.float32)
        position_distances = jnp.abs(homes - number.astype(jnp.float32))
        unnormalized_scores = jnp.einsum('gki,pki->kgp', memory_slot_query, window_block_keys) * score_scale - distance_slopes[:, None, None] * position_distances[None, :, None]
        local = lax.optimization_barrier(jnp.max(unnormalized_scores, axis=2))
        exponent_terms = jnp.exp(unnormalized_scores - local[:, :, None])
        part_den = lax.optimization_barrier(jnp.sum(exponent_terms, axis=2))
        attention_probabilities = lax.optimization_barrier(exponent_terms.astype(jnp.bfloat16)).astype(jnp.float32)
        partial_numerator = jnp.einsum('lca,alg->lcg', attention_probabilities, window_block_values)
        new_best = jnp.maximum(best, local)
        old_weight = jnp.exp(best - new_best)
        new_weight = jnp.exp(local - new_best)
        den = old_weight * den + new_weight * part_den
        num = old_weight[:, :, None] * num + new_weight[:, :, None] * partial_numerator
        return ((new_best, den, num), None)
    start_carry = (jnp.full((H, MEM), MASKED, jnp.float32), jnp.zeros((H, MEM), jnp.float32), jnp.zeros((H, MEM, HD), jnp.float32))
    (best, den, num), unused = lax.scan(slot_block, start_carry, jnp.arange(N_SEQ, dtype=jnp.int32))
    slot_mix = jnp.transpose(num / den[:, :, None], (1, 0, 2)).astype(jnp.bfloat16).reshape(MEM, D)
    mixed = jnp.concatenate([token_mix, slot_mix], axis=0)
    group = D // N_TENSOR
    summed = jnp.zeros((SEQ + MEM, D), jnp.float32)
    for index in range(N_TENSOR):
        part = jnp.dot(mixed[:, index * group:(index + 1) * group], w_output[index * group:(index + 1) * group], preferred_element_type=jnp.float32)
        summed = summed + lax.optimization_barrier(part.astype(jnp.bfloat16)).astype(jnp.float32)
    merged = rows.astype(jnp.float32) + summed
    mean_sq = lax.optimization_barrier(jnp.mean(merged * merged, axis=1, keepdims=True))
    normalized = (merged * lax.rsqrt(mean_sq + EPS) * norm_gain[None, :]).astype(jnp.bfloat16)
    new_state = jnp.where((remaining > 0)[:, None], normalized[:SEQ], state)
    new_memory = normalized[SEQ:]
    return (new_state, new_memory)
```

```python
import functools
import math

import jax
import jax.numpy as jnp
from jax import lax
from jax.experimental import pallas as pl
from jax.experimental.pallas import tpu as pltpu
from jax.sharding import PartitionSpec as P

H = 16
HD = 128
HALF = 256
EPS = 1e-05
MASKED = -1e30
F32 = jnp.float32
BF16 = jnp.bfloat16
CHUNK = 256


def kernel(
    n_seq, n_tensor,
    state, memory, wq, wk, wv, wo, gain, remaining, homes,
    new_state, new_memory,
    rows, wqkv, wob, q, k, v, mask, mixed,
    num, stat, numr, statr,
    tosend, pr, own, xsend, xr, res, sqs, sqr, sqms, sqmr,
    w_send, w_recv, s_send, s_recv, h_send, h_recv, m_send, m_recv, l_sem,
    p_send, p_recv, c_send, c_recv, x_send, x_recv, q_send, q_recv,
):
    tok, width = state.shape
    srows = memory.shape[0]
    slots = homes.shape[1]
    heads = width // HD
    D = rows.shape[1]
    depth = wq.shape[0]
    bw = wo.shape[1]
    outer, X = n_seq // 2, n_tensor // 2
    nch = tok // CHUNK
    s = lax.axis_index("seq")
    t = lax.axis_index("tensor")
    o, i = s // 2, s % 2
    x, c = t // 2, t % 2
    mate = x * 2 + 1 - c
    scale = 1.0 / math.sqrt(HD)
    base_slot = HALF + tok + HALF

    def remote(src, dst, ss, rs, seq, ten):
        return pltpu.make_async_remote_copy(
            src_ref=src, dst_ref=dst, send_sem=ss, recv_sem=rs,
            device_id=(seq, ten), device_id_type=pl.DeviceIdType.MESH,
        )

    barrier = pltpu.get_barrier_semaphore()
    for d in range(1, n_seq):
        pl.semaphore_signal(barrier, inc=1, device_id=((s + d) % n_seq, t), device_id_type=pl.DeviceIdType.MESH)
    for d in range(1, n_tensor):
        pl.semaphore_signal(barrier, inc=1, device_id=(s, (t + d) % n_tensor), device_id_type=pl.DeviceIdType.MESH)
    pl.semaphore_wait(barrier, n_seq + n_tensor - 2)

    cols = pl.ds(pl.multiple_of(t * width, width), width)

    pieces = [(HALF + p * CHUNK, CHUNK) for p in range(nch)]
    pieces += [(0, HALF), (HALF + tok, HALF), (base_slot, slots)]
    BEFORE, AFTER, SLOTS = nch, nch + 1, nch + 2

    def piece_on(p):
        if p == BEFORE:
            return s > 0
        if p == AFTER:
            return s < n_seq - 1
        return None

    def when(cond, f):
        if cond is None:
            f()
        else:
            pl.when(cond)(f)

    def piece_ref(p, who):
        start, size = pieces[p]
        return rows.at[pl.ds(start, size), pl.ds(pl.multiple_of(who * width, width), width)]

    def piece_copy(p, owner, lane, seq_to_ten):
        ref = piece_ref(p, owner)
        return remote(ref, ref, s_send.at[p, lane], s_recv.at[p, owner], s, seq_to_ten)

    def piece_out(p):
        def go():
            for d in range(1, X):
                piece_copy(p, t, d, ((x + d) % X) * 2 + c).start()
            piece_copy(p, t, 0, mate).start()
        when(piece_on(p), go)

    def piece_forward(p):
        def go():
            for d in range(1, X):
                owner = ((x + X - d) % X) * 2 + c
                piece_copy(p, owner, 0, mate).wait_recv()
                piece_copy(p, owner, X - 1 + d, mate).start()
        when(piece_on(p), go)

    def piece_in(p):
        def go():
            for d in range(X):
                piece_copy(p, ((x + d) % X) * 2 + 1 - c, 0, mate).wait_recv()
        when(piece_on(p), go)

    def piece_end(p):
        def go():
            for lane in range(2 * X - 1):
                piece_copy(p, t, lane, mate).wait_send()
        when(piece_on(p), go)

    def w_own(w):
        return (wk, wv, wq, wo)[w]

    def w_ref(w, b):
        if w == 3:
            return wob.at[b]
        return wqkv.at[w, pl.ds(pl.multiple_of(b * depth, depth), depth)]

    def w_copy(w, b, way, to):
        ref = w_ref(w, b)
        return remote(ref, ref, w_send.at[w, way, b], w_recv.at[w, b], to, t)

    def w_start(w):
        ref, mine = w_own(w), w_ref(w, s)
        for way, to, on in ((2, o * 2 + 1 - i, None), (0, s + 2, o < outer - 1), (1, s - 2, o > 0)):
            def go(way=way, to=to):
                remote(ref, mine, w_send.at[w, way, s], w_recv.at[w, s], to, t).start()
            when(on, go)
        pltpu.make_async_copy(ref, mine, l_sem.at[w]).start()

    def w_step(w, n):
        low, high = s - 2 * n, s + 2 * n

        @pl.when(o - n >= 0)
        def _():
            w_copy(w, low, 0, s).wait_recv()
            pl.when(o < outer - 1)(lambda: w_copy(w, low, 0, s + 2).start())
            w_copy(w, low, 2, o * 2 + 1 - i).start()

        @pl.when(o + n < outer)
        def _():
            w_copy(w, high, 0, s).wait_recv()
            pl.when(o > 0)(lambda: w_copy(w, high, 1, s - 2).start())
            w_copy(w, high, 2, o * 2 + 1 - i).start()

    def w_finish(w):
        for b in range(outer):
            w_copy(w, b * 2 + 1 - i, 0, s).wait_recv()
        pltpu.make_async_copy(w_own(w), w_ref(w, s), l_sem.at[w]).wait()

    def w_end(w):
        for b in range(outer):
            blk = b * 2 + i
            w_copy(w, blk, 2, s).wait_send()
            pl.when((o < outer - 1) & (b <= o))(lambda blk=blk: w_copy(w, blk, 0, s).wait_send())
            pl.when((o > 0) & (b >= o))(lambda blk=blk: w_copy(w, blk, 1, s).wait_send())

    def halo_copy(down):
        if down:
            return remote(state.at[pl.ds(0, HALF)], rows.at[pl.ds(HALF + tok, HALF), cols],
                          h_send.at[1], h_recv.at[1], s - 1, t)
        return remote(state.at[pl.ds(tok - HALF, HALF)], rows.at[pl.ds(0, HALF), cols],
                      h_send.at[0], h_recv.at[0], s + 1, t)

    def mem_copy(src, d, to):
        ref = rows.at[pl.ds(pl.multiple_of(base_slot + src * srows, srows), srows), cols]
        return remote(memory, ref, m_send.at[d], m_recv.at[src], to, t)

    for p in range(nch):
        def tok_copy(lane, to, p=p):
            return remote(state.at[pl.ds(p * CHUNK, CHUNK)], piece_ref(p, t),
                          s_send.at[p, lane], s_recv.at[p, t], s, to)
        for d in range(1, X):
            tok_copy(d, ((x + d) % X) * 2 + c).start()
    for p in range(nch):
        def tok_copy(lane, to, p=p):
            return remote(state.at[pl.ds(p * CHUNK, CHUNK)], piece_ref(p, t),
                          s_send.at[p, lane], s_recv.at[p, t], s, to)
        tok_copy(0, mate).start()
    for d in range(1, n_seq):
        mem_copy(s, d, (s + d) % n_seq).start()
    pl.when(s < n_seq - 1)(lambda: halo_copy(False).start())
    pl.when(s > 0)(lambda: halo_copy(True).start())
    w_start(0)
    rows[pl.ds(HALF, tok), cols] = state[...]
    rows[pl.ds(pl.multiple_of(base_slot + s * srows, srows), srows), cols] = memory[...]

    @pl.when(s == 0)
    def _():
        rows[pl.ds(0, HALF), :] = jnp.zeros((HALF, D), BF16)

    @pl.when(s == n_seq - 1)
    def _():
        rows[pl.ds(HALF + tok, HALF), :] = jnp.zeros((HALF, D), BF16)

    for d in range(1, n_seq):
        mem_copy((s + d) % n_seq, 0, s).wait_recv()
    piece_out(SLOTS)
    pl.when(s > 0)(lambda: halo_copy(False).wait_recv())
    piece_out(BEFORE)
    pl.when(s < n_seq - 1)(lambda: halo_copy(True).wait_recv())
    piece_out(AFTER)
    w_step(0, 1)
    w_start(1)
    piece_forward(0)
    piece_forward(1)
    for n in range(2, outer):
        w_step(0, n)
    for p in range(2, nch):
        piece_forward(p)
    piece_forward(SLOTS)
    piece_forward(BEFORE)
    piece_forward(AFTER)
    w_step(1, 1)
    w_start(2)
    for p in range(nch + 3):
        piece_in(p)
    w_finish(0)

    def project(w, dst, row, size, at):
        dst[pl.ds(at, size), :] = jnp.dot(
            rows[pl.ds(row, size), :], wqkv[w], preferred_element_type=F32
        ).astype(BF16)

    kv_rows = [(r * 2 * CHUNK, 2 * CHUNK) for r in range(base_slot // (2 * CHUNK))] + [(base_slot, slots)]
    q_rows = [(HALF + r * 2 * CHUNK, 2 * CHUNK) for r in range(tok // (2 * CHUNK))] + [(base_slot, slots)]

    def kv_project(w, dst, later, upto):
        for at, (row, size) in enumerate(kv_rows):
            project(w, dst, row, size, row)
            n = at + 2
            if n < outer:
                w_step(later, n)
        for n in range(len(kv_rows) + 2, outer):
            w_step(later, n)

    kv_project(0, k, 1, outer)
    w_step(2, 1)
    w_start(3)
    w_finish(1)
    kv_project(1, v, 2, outer)
    w_step(3, 1)
    w_finish(2)
    project(2, q, base_slot, slots, tok)
    for row, size in q_rows[:-1]:
        project(2, q, row, size, row - HALF)

    place = s.astype(F32)
    gap_row = jnp.abs(homes[...].astype(F32) - place)
    gap_col = jnp.transpose(jnp.broadcast_to(gap_row, (128, slots)))[:, 0:1]

    def slope(h, shape):
        order = jnp.full(shape, (t * heads + h).astype(F32), F32)
        return 0.25 * jnp.exp(order * (math.log(8.0) / (H - 1)))

    nt = (((1,), (1,)), ((), ()))
    lane = lax.broadcasted_iota(jnp.int32, (slots, 128), 1)
    packed = jnp.zeros((slots, 128), F32)
    for h in range(heads):
        hc = slice(h * HD, (h + 1) * HD)
        sc = lax.dot_general(q[pl.ds(tok, slots), hc], k[pl.ds(HALF, tok), hc], nt, preferred_element_type=F32)
        sc = sc * scale - slope(h, (slots, 1)) * gap_col
        top = jnp.max(sc, axis=1, keepdims=True)
        e = jnp.exp(sc - top)
        tot = jnp.sum(e, axis=1, keepdims=True)
        num[:, hc] = jnp.dot(e.astype(BF16), v[pl.ds(HALF, tok), hc], preferred_element_type=F32)
        packed = jnp.where(lane == h, top, packed)
        packed = jnp.where(lane == heads + h, tot, packed)
    stat[...] = packed

    def part_copy(which, src, d, to):
        a, b = ((num, numr), (stat, statr))[which]
        return remote(a.at[pl.ds(pl.multiple_of(to * srows, srows), srows)], b.at[src],
                      p_send.at[which, d], p_recv.at[which, src], to, t)

    for d in range(1, n_seq):
        for which in range(2):
            part_copy(which, s, d, (s + d) % n_seq).start()
    mine = pl.ds(pl.multiple_of(s * srows, srows), srows)
    numr[s] = num[mine, :]
    statr[s] = stat[mine, :]

    span = CHUNK + 2 * HALF

    def attend(j, carry):
        qq = lax.broadcasted_iota(jnp.int32, (CHUNK, span), 0)
        kk = lax.broadcasted_iota(jnp.int32, (CHUNK, span), 1)
        kpos = s * tok + j * CHUNK - HALF + kk
        ok = (kk >= qq) & (kk - qq <= 2 * HALF) & (kpos >= 0) & (kpos < tok * n_seq)
        mask[...] = jnp.where(ok, 0.0, MASKED)
        row = pl.multiple_of(j * CHUNK, CHUNK)
        for h in range(heads):
            hc = slice(h * HD, (h + 1) * HD)
            qh = q[pl.ds(row, CHUNK), hc]
            near = lax.dot_general(qh, k[pl.ds(row, span), hc], nt, preferred_element_type=F32)
            near = near * scale + mask[...]
            far = lax.dot_general(qh, k[pl.ds(base_slot, slots), hc], nt, preferred_element_type=F32)
            far = far * scale - slope(h, (1, slots)) * gap_row
            top = jnp.maximum(jnp.max(near, axis=1, keepdims=True), jnp.max(far, axis=1, keepdims=True))
            en = jnp.exp(near - top)
            ef = jnp.exp(far - top)
            tot = jnp.sum(en, axis=1, keepdims=True) + jnp.sum(ef, axis=1, keepdims=True)
            acc = jnp.dot(en.astype(BF16), v[pl.ds(row, span), hc], preferred_element_type=F32)
            acc = acc + jnp.dot(ef.astype(BF16), v[pl.ds(base_slot, slots), hc], preferred_element_type=F32)
            mixed[pl.ds(row, CHUNK), hc] = (acc / tot).astype(BF16)
        pl.when(j + 2 < outer)(lambda: w_step(3, j + 2))
        return carry

    lax.fori_loop(0, nch, attend, 0)
    for n in range(nch + 2, outer):
        w_step(3, n)

    for d in range(1, n_seq):
        for which in range(2):
            part_copy(which, (s + d) % n_seq, 0, s).wait_recv()
    for h in range(heads):
        hc = slice(h * HD, (h + 1) * HD)
        best = statr[0][:, h:h + 1]
        for b in range(1, n_seq):
            best = jnp.maximum(best, statr[b][:, h:h + 1])
        den = jnp.zeros((srows, 1), F32)
        acc = jnp.zeros((srows, HD), F32)
        for b in range(n_seq):
            weight = jnp.exp(statr[b][:, h:h + 1] - best)
            den = den + weight * statr[b][:, heads + h:heads + h + 1]
            acc = acc + weight * numr[b, :, hc]
        mixed[pl.ds(tok, srows), hc] = (acc / den).astype(BF16)
    w_finish(3)

    nb = width // bw
    outs = [(r * CHUNK, CHUNK) for r in range(nch)] + [(tok, srows)]

    def out_part(r, xd, core):
        row, size = outs[r]
        dest = xd * 2 + core
        a = mixed[pl.ds(row, size), :]
        return [jnp.dot(a, wob[dest * nb + b], preferred_element_type=F32).astype(BF16) for b in range(nb)]

    def core_copy(r, d):
        row, size = outs[r]
        return remote(tosend.at[d, pl.ds(row, size)], pr.at[d, pl.ds(row, size)],
                      c_send.at[r, d], c_recv.at[r, d], s, mate)

    def chip_copy(r, d):
        row, size = outs[r]
        return remote(xsend.at[d, pl.ds(row, size)], xr.at[d, pl.ds(row, size)],
                      x_send.at[r, d], x_recv.at[r, d], s, ((x + d) % X) * 2 + c)

    def store_parts(dst, d, r, parts):
        row, size = outs[r]
        for b, part in enumerate(parts):
            dst[d, pl.ds(row, size), b * bw:(b + 1) * bw] = part

    order = list(range(1, X)) + [0]
    for r in range(len(outs)):
        for d in order:
            store_parts(tosend, d, r, out_part(r, (x + d) % X, 1 - c))
            core_copy(r, d).start()
        for d in order:
            store_parts(xsend, d, r, out_part(r, (x + d) % X, c))
        row, size = outs[r]
        for d in range(1, X):
            core_copy(r, d).wait_recv()
            here = pl.ds(row, size)
            xsend[d, here, :] = (xsend[d, here, :].astype(F32) + pr[d, here, :].astype(F32)).astype(BF16)
            chip_copy(r, d).start()

    def sq_copy(r, d, owner, to):
        if r < nch:
            a, b = sqs.at[r], sqr.at[owner, r]
        else:
            a, b = sqms, sqmr.at[owner]
        return remote(a, b, q_send.at[r, d], q_recv.at[r, owner], s, to)

    for r, (row, size) in enumerate(outs):
        here = pl.ds(row, size)
        core_copy(r, 0).wait_recv()
        total = xsend[0, here, :].astype(F32) + pr[0, here, :].astype(F32)
        for d in range(1, X):
            chip_copy(r, d).wait_recv()
            total = total + xr[d, here, :].astype(F32)
        base = state[here, :] if r < nch else memory[...]
        total = base.astype(F32) + total
        res[here, :] = total
        sq = jnp.broadcast_to(jnp.sum(total * total, axis=1, keepdims=True), (size, 128))
        if r < nch:
            sqs[r] = jnp.transpose(sq)[0:8, :]
            sqr[t, r] = sqs[r]
        else:
            sqms[...] = sq
            sqmr[t] = sq
        for d in range(1, n_tensor):
            sq_copy(r, d, t, (t + d) % n_tensor).start()

    for r, (row, size) in enumerate(outs):
        here = pl.ds(row, size)
        for d in range(1, n_tensor):
            sq_copy(r, 0, (t + d) % n_tensor, t).wait_recv()
        if r < nch:
            sq = sqr[0, r]
            for b in range(1, n_tensor):
                sq = sq + sqr[b, r]
            sq = jnp.transpose(jnp.broadcast_to(sq[0:1, :], (128, size)))[:, 0:1]
        else:
            sq = sqmr[0]
            for b in range(1, n_tensor):
                sq = sq + sqmr[b]
            sq = sq[:, 0:1]
        out = (res[here, :] * lax.rsqrt(sq / D + EPS) * gain[...]).astype(BF16)
        if r < nch:
            left = jnp.broadcast_to(remaining[r:r + 1, :].astype(F32), (128, size))
            live = jnp.transpose(left)[:, 0:1] > 0.5
            new_state[here, :] = jnp.where(live, out.astype(F32), state[here, :].astype(F32)).astype(BF16)
        else:
            new_memory[...] = out

    for w in range(4):
        w_end(w)
    for p in range(nch + 3):
        piece_end(p)
    pl.when(s < n_seq - 1)(lambda: halo_copy(False).wait_send())
    pl.when(s > 0)(lambda: halo_copy(True).wait_send())
    for d in range(1, n_seq):
        mem_copy(s, d, (s + d) % n_seq).wait_send()
        for which in range(2):
            part_copy(which, s, d, (s + d) % n_seq).wait_send()
    for r in range(len(outs)):
        for d in range(X):
            core_copy(r, d).wait_send()
            if d:
                chip_copy(r, d).wait_send()
        for d in range(1, n_tensor):
            sq_copy(r, d, t, (t + d) % n_tensor).wait_send()


def shards(state, memory, w_query, w_key, w_value, w_output, norm_gain, remaining, slot_home):
    n_seq, n_tensor = lax.axis_size("seq"), lax.axis_size("tensor")
    tok, width = state.shape
    srows = memory.shape[0]
    slots = slot_home.shape[0]
    D = width * n_tensor
    X = n_tensor // 2
    nch = tok // CHUNK
    bw = w_output.shape[1]
    R = tok + 2 * HALF + slots
    dma = pltpu.SemaphoreType.DMA
    V = pltpu.VMEM
    return pl.pallas_call(
        functools.partial(kernel, n_seq, n_tensor),
        out_shape=(jax.ShapeDtypeStruct(state.shape, BF16), jax.ShapeDtypeStruct(memory.shape, BF16)),
        in_specs=[pl.BlockSpec(memory_space=V)] * 9,
        out_specs=(pl.BlockSpec(memory_space=V),) * 2,
        scratch_shapes=[
            V((R, D), BF16), V((3, D, width), BF16), V((n_seq, width, bw), BF16),
            V((tok + slots, width), BF16), V((R, width), BF16), V((R, width), BF16),
            V((CHUNK, CHUNK + 2 * HALF), F32), V((tok + srows, width), BF16),
            V((slots, width), F32), V((slots, 128), F32),
            V((n_seq, srows, width), F32), V((n_seq, srows, 128), F32),
            V((X, tok + srows, width), BF16), V((X, tok + srows, width), BF16), V((8, 128), BF16),
            V((X, tok + srows, width), BF16), V((X, tok + srows, width), BF16),
            V((tok + srows, width), F32),
            V((nch, 8, CHUNK), F32), V((n_tensor, nch, 8, CHUNK), F32),
            V((srows, 128), F32), V((n_tensor, srows, 128), F32),
            dma((4, 3, n_seq)), dma((4, n_seq)),
            dma((nch + 3, 2 * X - 1)), dma((nch + 3, n_tensor)),
            dma((2,)), dma((2,)), dma((n_seq,)), dma((n_seq,)), dma((4,)),
            dma((2, n_seq)), dma((2, n_seq)),
            dma((nch + 1, X)), dma((nch + 1, X)), dma((nch + 1, X)), dma((nch + 1, X)),
            dma((nch + 1, n_tensor)), dma((nch + 1, n_tensor)),
        ],
        compiler_params=pltpu.CompilerParams(
            collective_id=0, has_side_effects=True, vmem_limit_bytes=60 * 1024 * 1024
        ),
        cost_estimate=pl.CostEstimate(flops=12_000_000_000, bytes_accessed=8_000_000, transcendentals=4_000_000),
    )(
        state, memory, w_query, w_key, w_value, w_output,
        norm_gain.reshape(1, width), remaining.reshape(nch, CHUNK), slot_home.reshape(1, slots),
    )


def solution(mesh):
    placed = (
        P("seq", "tensor"), P("seq", "tensor"), P("seq", "tensor"), P("seq", "tensor"),
        P("seq", "tensor"), P("tensor", "seq"), P("tensor"), P("seq"), P(),
    )
    return jax.shard_map(
        shards, mesh=mesh, in_specs=placed,
        out_specs=(P("seq", "tensor"), P("seq", "tensor")), check_vma=False,
    )
```

```python
import functools
import math

import jax
import jax.numpy as jnp
from jax import lax
from jax.experimental import pallas as pl
from jax.experimental.pallas import tpu as pltpu
from jax.sharding import PartitionSpec as P

H = 16
HD = 128
HALF = 256
EPS = 1e-05
MASKED = -1e30
F32 = jnp.float32
BF16 = jnp.bfloat16
CHUNK = 256


def kernel(
    n_seq, n_tensor,
    state, memory, wq, wk, wv, wo, gain, remaining, homes,
    new_state, new_memory,
    rows, wqkv, wob, q, k, v, mask, mixed,
    num, stat, numr, statr,
    tosend, pr, xsend, xr, res, sqs, sqr, sqms, sqmr,
    w_send, w_recv, s_send, s_recv, h_send, h_recv, m_send, m_recv, l_sem,
    p_send, p_recv, c_send, c_recv, x_send, x_recv, q_send, q_recv,
):
    tok, width = state.shape
    srows = memory.shape[0]
    slots = homes.shape[1]
    heads = width // HD
    D = rows.shape[1]
    depth = wq.shape[0]
    bw = wo.shape[1]
    outer, X = n_seq // 2, n_tensor // 2
    nch = tok // CHUNK
    s = lax.axis_index("seq")
    t = lax.axis_index("tensor")
    o, i = s // 2, s % 2
    x, c = t // 2, t % 2
    mate = x * 2 + 1 - c
    scale = 1.0 / math.sqrt(HD)
    base_slot = HALF + tok + HALF

    def remote(src, dst, ss, rs, seq, ten):
        return pltpu.make_async_remote_copy(
            src_ref=src, dst_ref=dst, send_sem=ss, recv_sem=rs,
            device_id=(seq, ten), device_id_type=pl.DeviceIdType.MESH,
        )

    barrier = pltpu.get_barrier_semaphore()
    for d in range(1, n_seq):
        pl.semaphore_signal(barrier, inc=1, device_id=((s + d) % n_seq, t), device_id_type=pl.DeviceIdType.MESH)
    for d in range(1, n_tensor):
        pl.semaphore_signal(barrier, inc=1, device_id=(s, (t + d) % n_tensor), device_id_type=pl.DeviceIdType.MESH)
    pl.semaphore_wait(barrier, n_seq + n_tensor - 2)

    cols = pl.ds(pl.multiple_of(t * width, width), width)

    pieces = [(HALF + p * CHUNK, CHUNK) for p in range(nch)]
    pieces += [(0, HALF), (HALF + tok, HALF), (base_slot, slots)]
    BEFORE, AFTER, SLOTS = nch, nch + 1, nch + 2

    def piece_on(p):
        if p == BEFORE:
            return s > 0
        if p == AFTER:
            return s < n_seq - 1
        return None

    def when(cond, f):
        if cond is None:
            f()
        else:
            pl.when(cond)(f)

    def piece_ref(p, who):
        start, size = pieces[p]
        return rows.at[pl.ds(start, size), pl.ds(pl.multiple_of(who * width, width), width)]

    def piece_copy(p, owner, lane, seq_to_ten):
        ref = piece_ref(p, owner)
        return remote(ref, ref, s_send.at[p, lane], s_recv.at[p, owner], s, seq_to_ten)

    def piece_out(p):
        def go():
            for d in range(1, X):
                piece_copy(p, t, d, ((x + d) % X) * 2 + c).start()
            piece_copy(p, t, 0, mate).start()
        when(piece_on(p), go)

    def piece_forward(p):
        def go():
            for d in range(1, X):
                owner = ((x + X - d) % X) * 2 + c
                piece_copy(p, owner, 0, mate).wait_recv()
                piece_copy(p, owner, X - 1 + d, mate).start()
        when(piece_on(p), go)

    def piece_in(p):
        def go():
            for d in range(X):
                piece_copy(p, ((x + d) % X) * 2 + 1 - c, 0, mate).wait_recv()
        when(piece_on(p), go)

    def piece_end(p):
        def go():
            for lane in range(2 * X - 1):
                piece_copy(p, t, lane, mate).wait_send()
        when(piece_on(p), go)

    half = width // 2
    OUT = 6

    def w_own(w):
        if w == OUT:
            return wo
        return (wk, wv, wq)[w % 3].at[:, pl.ds((w // 3) * half, half)]

    def w_ref(w, b):
        if isinstance(w, int) and w == OUT:
            return wob.at[b]
        return wqkv.at[w, pl.ds(pl.multiple_of(b * depth, depth), depth)]

    def w_copy(w, b, way, to):
        ref = w_ref(w, b)
        return remote(ref, ref, w_send.at[w, way, b], w_recv.at[w, b], to, t)

    def w_start(w):
        ref, mine = w_own(w), w_ref(w, s)
        for way, to, on in ((2, o * 2 + 1 - i, None), (0, s + 2, o < outer - 1), (1, s - 2, o > 0)):
            def go(way=way, to=to):
                remote(ref, mine, w_send.at[w, way, s], w_recv.at[w, s], to, t).start()
            when(on, go)
        pltpu.make_async_copy(ref, mine, l_sem.at[w]).start()

    def w_step(w, n):
        low, high = s - 2 * n, s + 2 * n

        @pl.when(o - n >= 0)
        def _():
            w_copy(w, low, 0, s).wait_recv()
            pl.when(o < outer - 1)(lambda: w_copy(w, low, 0, s + 2).start())
            w_copy(w, low, 2, o * 2 + 1 - i).start()

        @pl.when(o + n < outer)
        def _():
            w_copy(w, high, 0, s).wait_recv()
            pl.when(o > 0)(lambda: w_copy(w, high, 1, s - 2).start())
            w_copy(w, high, 2, o * 2 + 1 - i).start()

    def w_finish(w):
        for b in range(outer):
            w_copy(w, b * 2 + 1 - i, 0, s).wait_recv()
        pltpu.make_async_copy(w_own(w), w_ref(w, s), l_sem.at[w]).wait()

    def w_end(w):
        for b in range(outer):
            blk = b * 2 + i
            w_copy(w, blk, 2, s).wait_send()
            pl.when((o < outer - 1) & (b <= o))(lambda blk=blk: w_copy(w, blk, 0, s).wait_send())
            pl.when((o > 0) & (b >= o))(lambda blk=blk: w_copy(w, blk, 1, s).wait_send())

    def halo_copy(down):
        if down:
            return remote(state.at[pl.ds(0, HALF)], rows.at[pl.ds(HALF + tok, HALF), cols],
                          h_send.at[1], h_recv.at[1], s - 1, t)
        return remote(state.at[pl.ds(tok - HALF, HALF)], rows.at[pl.ds(0, HALF), cols],
                      h_send.at[0], h_recv.at[0], s + 1, t)

    def mem_copy(src, d, to):
        ref = rows.at[pl.ds(pl.multiple_of(base_slot + src * srows, srows), srows), cols]
        return remote(memory, ref, m_send.at[d], m_recv.at[src], to, t)

    for p in range(nch):
        def tok_copy(lane, to, p=p):
            return remote(state.at[pl.ds(p * CHUNK, CHUNK)], piece_ref(p, t),
                          s_send.at[p, lane], s_recv.at[p, t], s, to)
        for d in range(1, X):
            tok_copy(d, ((x + d) % X) * 2 + c).start()
    for p in range(nch):
        def tok_copy(lane, to, p=p):
            return remote(state.at[pl.ds(p * CHUNK, CHUNK)], piece_ref(p, t),
                          s_send.at[p, lane], s_recv.at[p, t], s, to)
        tok_copy(0, mate).start()
    for d in range(1, n_seq):
        mem_copy(s, d, (s + d) % n_seq).start()
    pl.when(s < n_seq - 1)(lambda: halo_copy(False).start())
    pl.when(s > 0)(lambda: halo_copy(True).start())
    w_start(0)
    rows[pl.ds(HALF, tok), cols] = state[...]
    rows[pl.ds(pl.multiple_of(base_slot + s * srows, srows), srows), cols] = memory[...]

    @pl.when(s == 0)
    def _():
        rows[pl.ds(0, HALF), :] = jnp.zeros((HALF, D), BF16)

    @pl.when(s == n_seq - 1)
    def _():
        rows[pl.ds(HALF + tok, HALF), :] = jnp.zeros((HALF, D), BF16)

    for d in range(1, n_seq):
        mem_copy((s + d) % n_seq, 0, s).wait_recv()
    piece_out(SLOTS)
    pl.when(s > 0)(lambda: halo_copy(False).wait_recv())
    piece_out(BEFORE)
    pl.when(s < n_seq - 1)(lambda: halo_copy(True).wait_recv())
    piece_out(AFTER)
    steps = outer - 1
    issued = [0, 1]

    def start_upto(w):
        while issued[1] <= min(w, OUT):
            w_start(issued[1])
            issued[1] += 1

    def relay_one():
        g = issued[0]
        w, n = g // steps, 1 + g % steps
        if w > OUT:
            return
        start_upto(w)
        w_step(w, n)
        issued[0] += 1
        if n == 1:
            start_upto(w + 1)

    def relay_upto(w, n):
        while issued[0] < min(w, OUT + 1) * steps + n and issued[0] < (OUT + 1) * steps:
            relay_one()

    relay_upto(0, 1)
    piece_forward(0)
    piece_forward(1)
    relay_upto(1, 0)
    for p in range(2, nch):
        piece_forward(p)
    piece_forward(SLOTS)
    piece_forward(BEFORE)
    piece_forward(AFTER)
    relay_upto(1, 1)
    for p in range(nch + 3):
        piece_in(p)

    def project(w, dst, row, size, at):
        hc = slice((w // 3) * half, (w // 3 + 1) * half)
        dst[pl.ds(at, size), hc] = jnp.dot(
            rows[pl.ds(row, size), :], wqkv[w], preferred_element_type=F32
        ).astype(BF16)

    kv_rows = [(r * 2 * CHUNK, 2 * CHUNK) for r in range(base_slot // (2 * CHUNK))] + [(base_slot, slots)]
    q_rows = [(HALF + r * 2 * CHUNK, 2 * CHUNK) for r in range(tok // (2 * CHUNK))] + [(base_slot, slots)]

    def project_all(w):
        dst = (k, v, q)[w % 3]
        relay_upto(w + 1, 1)
        w_finish(w)
        for at, (row, size) in enumerate(q_rows if w % 3 == 2 else kv_rows):
            project(w, dst, row, size, row - HALF if w % 3 == 2 and row < base_slot else (tok if w % 3 == 2 else row))
            if at < 2 and w + 1 < OUT:
                relay_upto(w + 1, at + 2)

    place = s.astype(F32)
    gap_row = jnp.abs(homes[...].astype(F32) - place)
    gap_col = jnp.transpose(jnp.broadcast_to(gap_row, (128, slots)))[:, 0:1]

    def slope(h, shape):
        order = jnp.full(shape, (t * heads + h).astype(F32), F32)
        return 0.25 * jnp.exp(order * (math.log(8.0) / (H - 1)))

    nt = (((1,), (1,)), ((), ()))
    lane = lax.broadcasted_iota(jnp.int32, (slots, 128), 1)
    def slot_heads(which):
        packed = stat[...] if which else jnp.zeros((slots, 128), F32)
        for h in range(which * heads // 2, (which + 1) * heads // 2):
            hc = slice(h * HD, (h + 1) * HD)
            sc = lax.dot_general(q[pl.ds(tok, slots), hc], k[pl.ds(HALF, tok), hc], nt, preferred_element_type=F32)
            sc = sc * scale - slope(h, (slots, 1)) * gap_col
            top = jnp.max(sc, axis=1, keepdims=True)
            e = jnp.exp(sc - top)
            tot = jnp.sum(e, axis=1, keepdims=True)
            num[:, hc] = jnp.dot(e.astype(BF16), v[pl.ds(HALF, tok), hc], preferred_element_type=F32)
            packed = jnp.where(lane == h, top, packed)
            packed = jnp.where(lane == heads + h, tot, packed)
        stat[...] = packed

    def part_copy(which, src, d, to):
        a, b = ((num, numr), (stat, statr))[which]
        return remote(a.at[pl.ds(pl.multiple_of(to * srows, srows), srows)], b.at[src],
                      p_send.at[which, d], p_recv.at[which, src], to, t)

    def parts_out():
        for d in range(1, n_seq):
            for which in range(2):
                part_copy(which, s, d, (s + d) % n_seq).start()
        mine = pl.ds(pl.multiple_of(s * srows, srows), srows)
        numr[s] = num[mine, :]
        statr[s] = stat[mine, :]

    span = CHUNK + 2 * HALF

    def attend(which, relay, j, carry):
        qq = lax.broadcasted_iota(jnp.int32, (CHUNK, span), 0)
        kk = lax.broadcasted_iota(jnp.int32, (CHUNK, span), 1)
        kpos = s * tok + j * CHUNK - HALF + kk
        ok = (kk >= qq) & (kk - qq <= 2 * HALF) & (kpos >= 0) & (kpos < tok * n_seq)
        mask[...] = jnp.where(ok, 0.0, MASKED)
        row = pl.multiple_of(j * CHUNK, CHUNK)
        for h in range(which * heads // 2, (which + 1) * heads // 2):
            hc = slice(h * HD, (h + 1) * HD)
            qh = q[pl.ds(row, CHUNK), hc]
            near = lax.dot_general(qh, k[pl.ds(row, span), hc], nt, preferred_element_type=F32)
            near = near * scale + mask[...]
            far = lax.dot_general(qh, k[pl.ds(base_slot, slots), hc], nt, preferred_element_type=F32)
            far = far * scale - slope(h, (1, slots)) * gap_row
            top = jnp.maximum(jnp.max(near, axis=1, keepdims=True), jnp.max(far, axis=1, keepdims=True))
            en = jnp.exp(near - top)
            ef = jnp.exp(far - top)
            tot = jnp.sum(en, axis=1, keepdims=True) + jnp.sum(ef, axis=1, keepdims=True)
            acc = jnp.dot(en.astype(BF16), v[pl.ds(row, span), hc], preferred_element_type=F32)
            acc = acc + jnp.dot(ef.astype(BF16), v[pl.ds(base_slot, slots), hc], preferred_element_type=F32)
            mixed[pl.ds(row, CHUNK), hc] = (acc / tot).astype(BF16)
        relay(j)
        return carry

    for w in range(3):
        project_all(w)
    slot_heads(0)
    relay_upto(4, 1)
    start_upto(5)
    first = issued[0]

    def relay_early(j):
        g = first + j
        pl.when(g < OUT * steps)(lambda: w_step(g // steps, 1 + g % steps))

    lax.fori_loop(0, nch, functools.partial(attend, 0, relay_early), 0)
    issued[0] = min(first + nch, OUT * steps)
    start_upto(OUT)
    for w in range(3, 6):
        if w < 5:
            relay_upto(w + 1, 0)
        project_all(w)
    slot_heads(1)
    parts_out()
    late = issued[0] - OUT * steps + 1

    def relay_late(j):
        pl.when(j + late < outer)(lambda: w_step(OUT, j + late))

    lax.fori_loop(0, nch, functools.partial(attend, 1, relay_late), 0)
    for n in range(nch + late, outer):
        w_step(OUT, n)

    for d in range(1, n_seq):
        for which in range(2):
            part_copy(which, (s + d) % n_seq, 0, s).wait_recv()
    for h in range(heads):
        hc = slice(h * HD, (h + 1) * HD)
        best = statr[0][:, h:h + 1]
        for b in range(1, n_seq):
            best = jnp.maximum(best, statr[b][:, h:h + 1])
        den = jnp.zeros((srows, 1), F32)
        acc = jnp.zeros((srows, HD), F32)
        for b in range(n_seq):
            weight = jnp.exp(statr[b][:, h:h + 1] - best)
            den = den + weight * statr[b][:, heads + h:heads + h + 1]
            acc = acc + weight * numr[b, :, hc]
        mixed[pl.ds(tok, srows), hc] = (acc / den).astype(BF16)
    w_finish(OUT)

    nb = width // bw
    outs = [(r * CHUNK, CHUNK) for r in range(nch)] + [(tok, srows)]

    def out_part(r, xd, core):
        row, size = outs[r]
        dest = xd * 2 + core
        a = mixed[pl.ds(row, size), :]
        return [jnp.dot(a, wob[dest * nb + b], preferred_element_type=F32).astype(BF16) for b in range(nb)]

    def core_copy(r, d):
        row, size = outs[r]
        return remote(tosend.at[d, pl.ds(row, size)], pr.at[d, pl.ds(row, size)],
                      c_send.at[r, d], c_recv.at[r, d], s, mate)

    def chip_copy(r, d):
        row, size = outs[r]
        return remote(xsend.at[d, pl.ds(row, size)], xr.at[d, pl.ds(row, size)],
                      x_send.at[r, d], x_recv.at[r, d], s, ((x + d) % X) * 2 + c)

    def store_parts(dst, d, r, parts):
        row, size = outs[r]
        for b, part in enumerate(parts):
            dst[d, pl.ds(row, size), b * bw:(b + 1) * bw] = part

    order = list(range(1, X)) + [0]
    for r in range(len(outs)):
        for d in order:
            store_parts(tosend, d, r, out_part(r, (x + d) % X, 1 - c))
            core_copy(r, d).start()
        for d in order:
            store_parts(xsend, d, r, out_part(r, (x + d) % X, c))
        row, size = outs[r]
        for d in range(1, X):
            core_copy(r, d).wait_recv()
            here = pl.ds(row, size)
            xsend[d, here, :] = (xsend[d, here, :].astype(F32) + pr[d, here, :].astype(F32)).astype(BF16)
            chip_copy(r, d).start()

    def sq_copy(r, d, owner, to):
        if r < nch:
            a, b = sqs.at[r], sqr.at[owner, r]
        else:
            a, b = sqms, sqmr.at[owner]
        return remote(a, b, q_send.at[r, d], q_recv.at[r, owner], s, to)

    for r, (row, size) in enumerate(outs):
        here = pl.ds(row, size)
        core_copy(r, 0).wait_recv()
        total = xsend[0, here, :].astype(F32) + pr[0, here, :].astype(F32)
        for d in range(1, X):
            chip_copy(r, d).wait_recv()
            total = total + xr[d, here, :].astype(F32)
        base = state[here, :] if r < nch else memory[...]
        total = base.astype(F32) + total
        res[here, :] = total
        sq = jnp.broadcast_to(jnp.sum(total * total, axis=1, keepdims=True), (size, 128))
        if r < nch:
            sqs[r] = jnp.transpose(sq)[0:8, :]
            sqr[t, r] = sqs[r]
        else:
            sqms[...] = sq
            sqmr[t] = sq
        for d in range(1, n_tensor):
            sq_copy(r, d, t, (t + d) % n_tensor).start()

    for r, (row, size) in enumerate(outs):
        here = pl.ds(row, size)
        for d in range(1, n_tensor):
            sq_copy(r, 0, (t + d) % n_tensor, t).wait_recv()
        if r < nch:
            sq = sqr[0, r]
            for b in range(1, n_tensor):
                sq = sq + sqr[b, r]
            sq = jnp.transpose(jnp.broadcast_to(sq[0:1, :], (128, size)))[:, 0:1]
        else:
            sq = sqmr[0]
            for b in range(1, n_tensor):
                sq = sq + sqmr[b]
            sq = sq[:, 0:1]
        out = (res[here, :] * lax.rsqrt(sq / D + EPS) * gain[...]).astype(BF16)
        if r < nch:
            left = jnp.broadcast_to(remaining[r:r + 1, :].astype(F32), (128, size))
            live = jnp.transpose(left)[:, 0:1] > 0.5
            new_state[here, :] = jnp.where(live, out.astype(F32), state[here, :].astype(F32)).astype(BF16)
        else:
            new_memory[...] = out

    for w in range(OUT + 1):
        w_end(w)
    for p in range(nch + 3):
        piece_end(p)
    pl.when(s < n_seq - 1)(lambda: halo_copy(False).wait_send())
    pl.when(s > 0)(lambda: halo_copy(True).wait_send())
    for d in range(1, n_seq):
        mem_copy(s, d, (s + d) % n_seq).wait_send()
        for which in range(2):
            part_copy(which, s, d, (s + d) % n_seq).wait_send()
    for r in range(len(outs)):
        for d in range(X):
            core_copy(r, d).wait_send()
            if d:
                chip_copy(r, d).wait_send()
        for d in range(1, n_tensor):
            sq_copy(r, d, t, (t + d) % n_tensor).wait_send()


def shards(state, memory, w_query, w_key, w_value, w_output, norm_gain, remaining, slot_home):
    n_seq, n_tensor = lax.axis_size("seq"), lax.axis_size("tensor")
    tok, width = state.shape
    srows = memory.shape[0]
    slots = slot_home.shape[0]
    D = width * n_tensor
    X = n_tensor // 2
    nch = tok // CHUNK
    bw = w_output.shape[1]
    R = tok + 2 * HALF + slots
    dma = pltpu.SemaphoreType.DMA
    V = pltpu.VMEM
    return pl.pallas_call(
        functools.partial(kernel, n_seq, n_tensor),
        out_shape=(jax.ShapeDtypeStruct(state.shape, BF16), jax.ShapeDtypeStruct(memory.shape, BF16)),
        in_specs=[pl.BlockSpec(memory_space=V)] * 9,
        out_specs=(pl.BlockSpec(memory_space=V),) * 2,
        scratch_shapes=[
            V((R, D), BF16), V((6, D, width // 2), BF16), V((n_seq, width, bw), BF16),
            V((tok + slots, width), BF16), V((R, width), BF16), V((R, width), BF16),
            V((CHUNK, CHUNK + 2 * HALF), F32), V((tok + srows, width), BF16),
            V((slots, width), F32), V((slots, 128), F32),
            V((n_seq, srows, width), F32), V((n_seq, srows, 128), F32),
            V((X, tok + srows, width), BF16), V((X, tok + srows, width), BF16),
            V((X, tok + srows, width), BF16), V((X, tok + srows, width), BF16),
            V((tok + srows, width), F32),
            V((nch, 8, CHUNK), F32), V((n_tensor, nch, 8, CHUNK), F32),
            V((srows, 128), F32), V((n_tensor, srows, 128), F32),
            dma((7, 3, n_seq)), dma((7, n_seq)),
            dma((nch + 3, 2 * X - 1)), dma((nch + 3, n_tensor)),
            dma((2,)), dma((2,)), dma((n_seq,)), dma((n_seq,)), dma((7,)),
            dma((2, n_seq)), dma((2, n_seq)),
            dma((nch + 1, X)), dma((nch + 1, X)), dma((nch + 1, X)), dma((nch + 1, X)),
            dma((nch + 1, n_tensor)), dma((nch + 1, n_tensor)),
        ],
        compiler_params=pltpu.CompilerParams(
            collective_id=0, has_side_effects=True, vmem_limit_bytes=60 * 1024 * 1024
        ),
        cost_estimate=pl.CostEstimate(flops=12_000_000_000, bytes_accessed=8_000_000, transcendentals=4_000_000),
    )(
        state, memory, w_query, w_key, w_value, w_output,
        norm_gain.reshape(1, width), remaining.reshape(nch, CHUNK), slot_home.reshape(1, slots),
    )


def solution(mesh):
    placed = (
        P("seq", "tensor"), P("seq", "tensor"), P("seq", "tensor"), P("seq", "tensor"),
        P("seq", "tensor"), P("tensor", "seq"), P("tensor"), P("seq"), P(),
    )
    return jax.shard_map(
        shards, mesh=mesh, in_specs=placed,
        out_specs=(P("seq", "tensor"), P("seq", "tensor")), check_vma=False,
    )
```
